512 devices in a mesh: sta: 64 (over x_hi, z, core), win: 8 (over y, x_lo).
Axes of the slice: x: 4 (x_hi: 2, x_lo: 2; x = x_hi * 2 + x_lo), y: 4, z: 16, core: 2. Of those that a mesh axis runs over, the one named last changes fastest.
Arguments:
- phases: bfloat16 [64, 1024, 1024], P('win', 'sta'), may hold values from -3.140625 to 3.140625
- validity: int32 [64, 1024], P('win', 'sta'), may hold values from 0 to 1, as said below
- plan: int32 [4], replicated, may hold values from 0 to 63
Outputs:
- correlation: bfloat16 [4, 16, 1024, 256], P(None, 'win', 'sta')
The draws below stay inside these ranges and needn't reach their ends.
Inputs may be any that keep to these rules, and one draw needn't show every extreme that they name: `plan`: each entry names a block of 16 consecutive stations. `validity`: 0 or 1; some stations have no usable window at all.
All inputs are finite; a program needn't handle non-finite values.
Results may differ from the reference program's by a relative error of at most 0.015.
Values may be sent and summed in bfloat16 or wider, within the bound.
No kernel may reach another device: no remote copies, remote signals or barrier semaphores. Data moves between devices by JAX's collectives and lax.ppermute only.
A program may use at most 64 MiB of HBM per device.

```python
import math
import jax
import jax.numpy as jnp
from jax import lax

BINS = 1024
LAGS = 256
SRC = 16
STEPS = 4
WIN_DEV = 8
STATIONS = 1024
WINDOWS = 64
N_WIN = 8


def draw_validity(key, part):
    key = jax.random.fold_in(key, 7)
    first_key, second_key = jax.random.split(key)
    living = jax.random.randint(first_key, (1, STATIONS), 0, 16) != 0
    window_index = jnp.arange(WINDOWS, dtype=jnp.int32)[:, None]
    limit = 30 + 65 * window_index // max(WINDOWS - 1, 1)
    dice_roll = jax.random.randint(second_key, (WINDOWS, STATIONS), 0, 100)
    return ((dice_roll < limit) & living).astype(jnp.int32)


def set_ends(result, stream_key, low, largest):
    index_at = [jax.random.randint(jax.random.fold_in(stream_key, axis), (), 0, length) for axis, length in enumerate(result.shape)]
    main_axis = result.shape.index(max(result.shape))
    beside = index_at[:main_axis] + [(index_at[main_axis] + 1) % result.shape[main_axis]] + index_at[main_axis + 1:]
    return result.at[tuple(index_at)].set(low).at[tuple(beside)].set(largest)


def setup_inputs(seed: int = 0) -> dict:
    streams_of = jax.random.split(jax.random.key(seed), 4)
    return {
        "phases": jnp.clip(jax.random.uniform(streams_of[0], (WINDOWS, STATIONS, BINS), jnp.float32, -3.140625, 3.140625), -3.140625, 3.140625).astype(jnp.bfloat16),
        "validity": draw_validity(jax.random.fold_in(streams_of[3], 71), 0),
        "plan": set_ends(jax.random.randint(streams_of[2], (STEPS,), 0, STATIONS // SRC), jax.random.fold_in(streams_of[2], 1), 0, (STATIONS // SRC) - 1).astype(jnp.int32),
    }


def idft_table(bins, lags):
    frequency = jnp.arange(bins, dtype=jnp.int32)[:, None]
    lag_offset = jnp.arange(lags, dtype=jnp.int32)[None, :] - lags // 2
    phase_turns = jnp.mod(frequency * lag_offset, 2 * bins).astype(jnp.float32)
    angles = phase_turns * (math.pi / bins)
    return jnp.concatenate([jnp.cos(angles), -jnp.sin(angles)], 0).astype(jnp.bfloat16)

def whiten(phases, station_flags):
    values = phases.astype(jnp.float32)
    spectra = jnp.concatenate([jnp.cos(values), jnp.sin(values)], -1)
    return (spectra * station_flags[..., None]).astype(jnp.bfloat16)

def pair_product(left_side, right_side):
    return jnp.einsum('wsf,wrf->srf', left_side.astype(jnp.float32), right_side.astype(jnp.float32))

def cross_lags(source, receivers, lag_table):
    half_bins = source.shape[-1] // 2
    source_re, source_im = (source[..., :half_bins], source[..., half_bins:])
    recv_re, recv_im = (receivers[..., :half_bins], receivers[..., half_bins:])
    real_part = pair_product(source_re, recv_re) + pair_product(source_im, recv_im)
    imag_part = pair_product(source_im, recv_re) - pair_product(source_re, recv_im)
    stacked = jnp.concatenate([real_part, imag_part], -1).astype(jnp.bfloat16)
    flat = stacked.reshape(-1, 2 * half_bins)
    lagged = jnp.dot(flat, lag_table, preferred_element_type=jnp.float32)
    return lagged.reshape(source.shape[1], receivers.shape[1], lag_table.shape[1])

def reference(phases, validity, plan):
    lag_table = idft_table(BINS, LAGS)
    station_flags = validity.astype(jnp.float32)
    spectra = whiten(phases, station_flags)
    results = []
    for step_index in range(STEPS):
        start_row = (plan[step_index] * SRC).astype(jnp.int32)
        source = lax.dynamic_slice_in_dim(spectra, start_row, SRC, 1)
        source_flags = lax.dynamic_slice_in_dim(station_flags, start_row, SRC, 1)
        lag_sum = jnp.zeros((SRC, STATIONS, LAGS), jnp.float32)
        for group_index in range(N_WIN):
            lower = group_index * WIN_DEV
            upper = lower + WIN_DEV
            group_lags = cross_lags(source[lower:upper], spectra[lower:upper], lag_table).astype(jnp.bfloat16)
            group_lags = lax.optimization_barrier(group_lags)
            lag_sum = lag_sum + group_lags.astype(jnp.float32)
        pair_count = jnp.dot(source_flags.T, station_flags, precision=lax.Precision.HIGHEST)
        factor = 1.0 / (math.sqrt(BINS) * jnp.sqrt(jnp.maximum(pair_count, 1.0)))
        results.append((lag_sum * factor[..., None]).astype(jnp.bfloat16))
    return jnp.stack(results, 0)
```

```python
import math

import jax
import jax.numpy as jnp
from jax import lax
from jax.sharding import PartitionSpec as P

LAGS = 256
SRC = 16
STEPS = 4
N_Z = 16
N_WIN = 8
N_STA = 64
FLAG_LANES = 128

SAME_Z = [[32 * h + 2 * z + c for h in range(2) for c in range(2)] for z in range(N_Z)]
ALONG_Z = [[32 * h + 2 * z + c for z in range(N_Z)] for h in range(2) for c in range(2)]
QUADS = [
    [w * N_STA + 4 * i + j for w in range(N_WIN) for j in range(4)] for i in range(N_STA // 4)
]


def xor_pairs(size, mask):
    return [(i, i ^ mask) for i in range(size)]


def idft_table(bins, lags):
    frequency = jnp.arange(bins, dtype=jnp.int32)[:, None]
    lag_offset = jnp.arange(lags, dtype=jnp.int32)[None, :] - lags // 2
    phase_turns = jnp.mod(frequency * lag_offset, 2 * bins).astype(jnp.float32)
    angles = phase_turns * (math.pi / bins)
    return jnp.concatenate([jnp.cos(angles), -jnp.sin(angles)], 0).astype(jnp.bfloat16)


def spectra_of(rows, bins):
    values = rows[..., :bins].astype(jnp.float32)
    flags = rows[..., bins : bins + 1].astype(jnp.float32)
    return jnp.cos(values) * flags, jnp.sin(values) * flags, flags[..., 0]


def on_device(phases, validity, plan):
    windows_here, stations_here, bins = phases.shape
    width = bins + FLAG_LANES
    me = lax.axis_index("sta")
    quad_place = lax.rem(me, 4)
    core = lax.rem(me, 2)
    flags = jnp.broadcast_to(
        validity.astype(jnp.bfloat16)[..., None], (windows_here, stations_here, FLAG_LANES)
    )
    own = jnp.concatenate([phases, flags], -1)

    two = jnp.stack([own, lax.ppermute(own, "sta", xor_pairs(N_STA, 1))], 0)
    four = jnp.concatenate([two, lax.ppermute(two, "sta", xor_pairs(N_STA, 2))], 0)

    pieces = lax.all_to_all(
        own.reshape(N_Z, 8, width), "sta", 0, 0, tiled=True, axis_index_groups=ALONG_Z
    )
    owner_z = lax.rem(plan // 2, N_Z)
    owner_place = 2 * (plan // 32) + lax.rem(plan, 2)
    held = jnp.stack([lax.dynamic_index_in_dim(pieces, owner_z[k], 0, False) for k in range(STEPS)])
    by_core = held.reshape(2, 2, 8, width).transpose(1, 0, 2, 3)
    sent = jnp.broadcast_to(by_core[None], (2, 2, 2, 8, width)).reshape(4, 2, 8, width)
    came = lax.all_to_all(sent, "sta", 0, 0, tiled=True, axis_index_groups=SAME_Z)
    mine = jnp.stack(
        [
            lax.dynamic_slice(
                came, (owner_place[2 * half + core], half, 0, 0), (1, 1, 8, width)
            ).reshape(8, width)
            for half in range(2)
        ]
    )
    source = lax.all_to_all(
        jnp.tile(mine, (N_Z // 2, 1, 1)), "sta", 0, 0, tiled=True, axis_index_groups=ALONG_Z
    ).reshape(windows_here, SRC, width)

    src_re, src_im, src_flags = spectra_of(source, bins)
    receivers = four.transpose(1, 0, 2, 3)[:, quad_place ^ jnp.arange(4)].reshape(
        windows_here, 4 * stations_here, width
    )
    rec_re, rec_im, rec_flags = spectra_of(receivers, bins)

    def over_windows(one, two, three, four, sign):
        return jnp.sum(
            one[:, :, None] * two[:, None] + sign * (three[:, :, None] * four[:, None]), 0
        )

    real_part = over_windows(src_re, rec_re, src_im, rec_im, 1.0)
    imag_part = over_windows(src_im, rec_re, src_re, rec_im, -1.0)
    stacked = jnp.concatenate([real_part, imag_part], -1).astype(jnp.bfloat16)
    lagged = jnp.dot(
        stacked.reshape(-1, 2 * bins), idft_table(bins, LAGS), preferred_element_type=jnp.float32
    ).astype(jnp.bfloat16)
    counts = jnp.dot(
        src_flags.T.astype(jnp.bfloat16),
        rec_flags.astype(jnp.bfloat16),
        preferred_element_type=jnp.float32,
    ).astype(jnp.bfloat16)

    lag_pieces = lagged.reshape(N_WIN, 2, 4, stations_here, LAGS).transpose(0, 2, 1, 3, 4)
    lag_pieces = lag_pieces.reshape(N_WIN * 4, 2 * stations_here, LAGS)
    count_pieces = counts.reshape(N_WIN, 2, 4, stations_here).transpose(0, 2, 1, 3)
    count_pieces = count_pieces.reshape(N_WIN * 4, 2, stations_here)
    count_pieces = jnp.pad(count_pieces, ((0, 0), (0, 6), (0, LAGS - stations_here)))
    back = lax.all_to_all(
        jnp.concatenate([lag_pieces, count_pieces], 1),
        ("win", "sta"),
        0,
        0,
        tiled=True,
        axis_index_groups=QUADS,
    )
    total = jnp.sum(back.reshape(N_WIN, 4, 2 * stations_here + 8, LAGS).astype(jnp.float32), 0)
    lag_sum = total[:, : 2 * stations_here].reshape(STEPS, 2, stations_here, LAGS)
    pair_count = total[:, 2 * stations_here : 2 * stations_here + 2, :stations_here]
    factor = 1.0 / (math.sqrt(bins) * jnp.sqrt(jnp.maximum(pair_count, 1.0)))
    return (lag_sum * factor[..., None]).astype(jnp.bfloat16)


def solution(mesh):
    return jax.shard_map(
        on_device,
        mesh=mesh,
        in_specs=(P("win", "sta", None), P("win", "sta"), P()),
        out_specs=P(None, "win", "sta", None),
        check_vma=False,
    )
```

```python
import math

import jax
import jax.numpy as jnp
from jax import lax
from jax.experimental import pallas as pl
from jax.experimental.pallas import tpu as pltpu
from jax.sharding import PartitionSpec as P

BINS = 1024
LAGS = 256
SRC = 16
STEPS = 4
WIN_DEV = 8
N_Z = 16
N_WIN = 8
N_STA = 64
LANES = 128
CHUNKS = BINS // LANES
WIDTH = BINS + LANES
PIECE_ROWS = 72

QUAD = [[32 * h + 2 * z + c for h in range(2) for c in range(2)] for z in range(N_Z)]
ALONG_Z = [[32 * h + 2 * z + c for z in range(N_Z)] for h in range(2) for c in range(2)]
ALL_QUADS = [[w * N_STA + i for w in range(N_WIN) for i in quad] for quad in QUAD]
MASKS = (0, 2, 1, 3)

SINE = (
    0.7071067690849304,
    -0.029462749138474464,
    0.0003682656097225845,
    -2.1877108338230755e-06,
    7.1552790359419305e-09,
)
COSINE = (
    1.4142135381698608,
    -0.17677636444568634,
    0.003682575421407819,
    -3.061264942516573e-05,
    1.2790856374067516e-07,
)


def xor_pairs(mask):
    return [(i, i ^ mask) for i in range(N_STA)]


def idft_table(bins, lags):
    frequency = jnp.arange(bins, dtype=jnp.int32)[:, None]
    lag_offset = jnp.arange(lags, dtype=jnp.int32)[None, :] - lags // 2
    phase_turns = jnp.mod(frequency * lag_offset, 2 * bins).astype(jnp.float32)
    angles = phase_turns * (math.pi / bins)
    return jnp.concatenate([jnp.cos(angles), -jnp.sin(angles)], 0).astype(jnp.bfloat16)


def cos_sin(x):
    square = x * x
    sine, cosine = SINE[-1], COSINE[-1]
    for a, b in zip(SINE[-2::-1], COSINE[-2::-1]):
        sine = sine * square + a
        cosine = cosine * square + b
    sine = sine * x
    return 1.0 - sine * sine, sine * cosine


def receivers_kernel(one_ref, two_ref, re_ref, im_ref, flag_ref):
    lanes = lax.broadcasted_iota(jnp.int32, (SRC, LANES), 1)
    for group, ref in enumerate((one_ref, two_ref)):
        for place in range(2):
            rows = slice(32 * group + SRC * place, 32 * group + SRC * place + SRC)

            def window(w, marks):
                flag = ref[place, w, :, BINS:].astype(jnp.float32)
                for c in range(CHUNKS):
                    cols = slice(LANES * c, LANES * c + LANES)
                    re, im = cos_sin(ref[place, w, :, cols].astype(jnp.float32))
                    re_ref[w, rows, cols] = (re * flag).astype(jnp.bfloat16)
                    im_ref[w, rows, cols] = (im * flag).astype(jnp.bfloat16)
                return marks + jnp.where(lanes == w, flag, 0.0)

            marks = lax.fori_loop(0, WIN_DEV, window, jnp.zeros((SRC, LANES), jnp.float32))
            flag_ref[rows, :] = marks.astype(jnp.bfloat16)


def receivers(one, two):
    spectrum = jax.ShapeDtypeStruct((WIN_DEV, 4 * SRC, BINS), jnp.bfloat16)
    return pl.pallas_call(
        receivers_kernel,
        out_shape=[spectrum, spectrum, jax.ShapeDtypeStruct((4 * SRC, LANES), jnp.bfloat16)],
        compiler_params=pltpu.CompilerParams(vmem_limit_bytes=32 << 20),
        cost_estimate=pl.CostEstimate(
            flops=25 * 4 * SRC * WIN_DEV * BINS, bytes_accessed=4 << 20, transcendentals=0
        ),
        name="receivers",
    )(one, two)


def correlate_kernel(
    place_ref, src_ref, re_ref, im_ref, flag_ref, table_ref, out_ref, src_re, src_im, stacked
):
    lanes = lax.broadcasted_iota(jnp.int32, (SRC, LANES), 1)
    place = place_ref[0]
    marks = jnp.zeros((SRC, LANES), jnp.float32)
    for w in range(WIN_DEV):
        flag = src_ref[SRC * w : SRC * w + SRC, BINS:].astype(jnp.float32)
        marks = marks + jnp.where(lanes == w, flag, 0.0)
    marks = marks.astype(jnp.bfloat16)

    def prepare(c, carry):
        cols = pl.ds(pl.multiple_of(c * LANES, LANES), LANES)
        for w in range(WIN_DEV):
            rows = slice(SRC * w, SRC * w + SRC)
            flag = src_ref[rows, BINS:].astype(jnp.float32)
            re, im = cos_sin(src_ref[rows, cols].astype(jnp.float32))
            re, im = re * flag, im * flag
            for s in range(SRC):
                wide = (SRC, LANES)
                src_re[c, SRC * w + s] = jnp.broadcast_to(re[s : s + 1], wide).astype(jnp.bfloat16)
                src_im[c, SRC * w + s] = jnp.broadcast_to(im[s : s + 1], wide).astype(jnp.bfloat16)
        return carry

    lax.fori_loop(0, CHUNKS, prepare, 0)
    for half in range(2):

        def chunk(c, carry):
            cols = pl.ds(pl.multiple_of(c * LANES, LANES), LANES)
            later = pl.ds(pl.multiple_of(BINS + c * LANES, LANES), LANES)
            blocks = [slice(32 * half + SRC * h, 32 * half + SRC * h + SRC) for h in range(2)]
            rec_re = [[re_ref[w, rows, cols] for rows in blocks] for w in range(WIN_DEV)]
            rec_im = [[im_ref[w, rows, cols] for rows in blocks] for w in range(WIN_DEV)]
            for s in range(SRC):
                real, imag = [[], []], [[], []]
                for w in range(WIN_DEV):
                    a, b = src_re[c, SRC * w + s], src_im[c, SRC * w + s]
                    for h in range(2):
                        real[h].append(a * rec_re[w][h] + b * rec_im[w][h])
                        imag[h].append(b * rec_re[w][h] - a * rec_im[w][h])
                for h in range(2):
                    for terms, place_of in ((real[h], cols), (imag[h], later)):
                        while len(terms) > 1:
                            terms = [terms[i] + terms[i + 1] for i in range(0, len(terms), 2)]
                        stacked[2 * half + h, SRC * s : SRC * s + SRC, place_of] = terms[0]
            return carry

        lax.fori_loop(0, CHUNKS, chunk, 0)
    for d in range(4):
        lags = jnp.dot(stacked[d], table_ref[...], preferred_element_type=jnp.float32)
        lags = lags.astype(jnp.bfloat16)
        count = lax.dot_general(
            marks,
            flag_ref[SRC * d : SRC * d + SRC, :],
            (((1,), (1,)), ((), ())),
            preferred_element_type=jnp.float32,
        )
        count = jnp.concatenate([count, jnp.zeros((SRC, LANES - SRC), jnp.float32)], 1)
        count = count.astype(jnp.bfloat16)
        to = place ^ MASKS[d]
        for w in range(N_WIN):
            out_ref[w, to, 0:32, :] = lags[32 * w : 32 * w + 32, :LANES]
            out_ref[w, to, 32:64, :] = lags[32 * w : 32 * w + 32, LANES:]
            first = 8 * (w // 4)
            out_ref[w, to, 64:PIECE_ROWS, :] = count[first : first + 8]


def correlate(place, source, rec_re, rec_im, rec_flags, table):
    vmem = pl.BlockSpec(memory_space=pltpu.VMEM)
    return pl.pallas_call(
        correlate_kernel,
        out_shape=jax.ShapeDtypeStruct((N_WIN, 4, PIECE_ROWS, LANES), jnp.bfloat16),
        in_specs=[pl.BlockSpec(memory_space=pltpu.SMEM)] + [vmem] * 5,
        out_specs=vmem,
        scratch_shapes=[pltpu.VMEM((CHUNKS, WIN_DEV * SRC, SRC, LANES), jnp.bfloat16)] * 2
        + [pltpu.VMEM((4, SRC * SRC, 2 * BINS), jnp.bfloat16)],
        compiler_params=pltpu.CompilerParams(vmem_limit_bytes=40 << 20),
        cost_estimate=pl.CostEstimate(flops=1 << 30, bytes_accessed=4 << 20, transcendentals=0),
        name="correlate",
    )(place, source, rec_re, rec_im, rec_flags, table)


def on_device(phases, validity, plan):
    me = lax.axis_index("sta")
    place = 2 * (me // 32) + lax.rem(me, 2)
    flags = jnp.broadcast_to(
        validity.astype(jnp.bfloat16)[..., None], (WIN_DEV, SRC, LANES)
    )
    own = jnp.concatenate([phases, flags], -1)

    one = jnp.stack([own, lax.ppermute(own, "sta", xor_pairs(32))], 0)
    two = lax.ppermute(one, "sta", xor_pairs(1))
    rec_re, rec_im, rec_flags = receivers(one, two)

    pieces = lax.all_to_all(
        own.reshape(N_Z, 8, WIDTH), "sta", 0, 0, tiled=True, axis_index_groups=ALONG_Z
    )
    owner_z = lax.rem(plan // 2, N_Z)
    owner_place = 2 * (plan // 32) + lax.rem(plan, 2)
    held = jnp.stack(
        [lax.dynamic_index_in_dim(pieces, owner_z[k], 0, False) for k in range(STEPS)]
    )
    came = lax.all_to_all(held, "sta", 0, 0, tiled=True, axis_index_groups=QUAD)
    mine = lax.dynamic_slice_in_dim(came, owner_place[place], 1, 0)
    source = lax.all_to_all(
        jnp.broadcast_to(mine, (N_Z, 8, WIDTH)),
        "sta",
        0,
        0,
        tiled=True,
        axis_index_groups=ALONG_Z,
    ).reshape(WIN_DEV * SRC, WIDTH)

    sent = correlate(place[None], source, rec_re, rec_im, rec_flags, idft_table(BINS, LAGS))
    back = lax.all_to_all(
        sent.reshape(N_WIN * 4, PIECE_ROWS, LANES),
        ("win", "sta"),
        0,
        0,
        tiled=True,
        axis_index_groups=ALL_QUADS,
    )
    total = jnp.sum(back.reshape(N_WIN, 4, PIECE_ROWS, LANES).astype(jnp.float32), 0)
    lag_sum = total[:, :64].reshape(STEPS, 2, 2, SRC, LANES).transpose(0, 2, 3, 1, 4)
    lag_sum = lag_sum.reshape(STEPS, 2, SRC, LAGS)
    first = 64 + 2 * lax.rem(lax.axis_index("win"), 4)
    pair_count = lax.dynamic_slice(total, (0, first, 0), (STEPS, 2, SRC))
    factor = 1.0 / (math.sqrt(BINS) * jnp.sqrt(jnp.maximum(pair_count, 1.0)))
    return (lag_sum * factor[..., None]).astype(jnp.bfloat16)


def solution(mesh):
    return jax.shard_map(
        on_device,
        mesh=mesh,
        in_specs=(P("win", "sta", None), P("win", "sta"), P()),
        out_specs=P(None, "win", "sta", None),
        check_vma=False,
    )
```

```python
import math

import jax
import jax.numpy as jnp
from jax import lax
from jax.experimental import pallas as pl
from jax.experimental.pallas import tpu as pltpu
from jax.sharding import PartitionSpec as P

BINS = 1024
LAGS = 256
SRC = 16
STEPS = 4
WIN_DEV = 8
N_Z = 16
N_WIN = 8
N_STA = 64
LANES = 128
CHUNKS = BINS // LANES
WIDTH = BINS + LANES
PIECE_ROWS = 72

QUAD = [[32 * h + 2 * z + c for h in range(2) for c in range(2)] for z in range(N_Z)]
ALONG_Z = [[32 * h + 2 * z + c for z in range(N_Z)] for h in range(2) for c in range(2)]
ALL_QUADS = [
    [w * N_STA + 32 * h + 2 * z + c for w in range(N_WIN) for h in range(2) for c in range(2)]
    for z in range(N_Z)
]
MASKS = (0, 2, 1, 3)

SINE = (
    0.7071067690849304,
    -0.029462749138474464,
    0.0003682656097225845,
    -2.1877108338230755e-06,
    7.1552790359419305e-09,
)
COSINE = (
    1.4142135381698608,
    -0.17677636444568634,
    0.003682575421407819,
    -3.061264942516573e-05,
    1.2790856374067516e-07,
)


def xor_pairs(mask):
    return [(i, i ^ mask) for i in range(N_STA)]


def idft_table(bins, lags):
    frequency = jnp.arange(bins, dtype=jnp.int32)[:, None]
    lag_offset = jnp.arange(lags, dtype=jnp.int32)[None, :] - lags // 2
    phase_turns = jnp.mod(frequency * lag_offset, 2 * bins).astype(jnp.float32)
    angles = phase_turns * (math.pi / bins)
    return jnp.concatenate([jnp.cos(angles), -jnp.sin(angles)], 0).astype(jnp.bfloat16)


def cos_sin(x):
    square = x * x
    sine, cosine = SINE[-1], COSINE[-1]
    for a, b in zip(SINE[-2::-1], COSINE[-2::-1]):
        sine = sine * square + a
        cosine = cosine * square + b
    sine = sine * x
    return 1.0 - sine * sine, sine * cosine


def pack_kernel(phases_ref, validity_ref, out_ref):
    flags = validity_ref[...].astype(jnp.float32)
    here = lax.broadcasted_iota(jnp.int32, (SRC, SRC), 0)
    here = here == lax.broadcasted_iota(jnp.int32, (SRC, SRC), 1)
    for w in range(WIN_DEV):
        rows = slice(SRC * w, SRC * w + SRC)
        out_ref[rows, :BINS] = phases_ref[w]
        row = jnp.broadcast_to(flags[w : w + 1], (SRC, SRC))
        column = jnp.sum(jnp.where(here, row, 0.0), 1, keepdims=True)
        out_ref[rows, BINS:] = jnp.broadcast_to(column, (SRC, LANES)).astype(jnp.bfloat16)


def pack(phases, validity):
    return pl.pallas_call(
        pack_kernel,
        out_shape=jax.ShapeDtypeStruct((WIN_DEV * SRC, WIDTH), jnp.bfloat16),
        cost_estimate=pl.CostEstimate(flops=0, bytes_accessed=600 << 10, transcendentals=0),
        name="pack",
    )(phases, validity)


def receivers_kernel(one_ref, two_ref, re_ref, im_ref, flag_ref):
    lanes = lax.broadcasted_iota(jnp.int32, (SRC, LANES), 1)
    for group, ref in enumerate((one_ref, two_ref)):
        for place in range(2):
            rows = slice(32 * group + SRC * place, 32 * group + SRC * place + SRC)

            def window(w, marks):
                flag = ref[place, w, :, BINS:].astype(jnp.float32)
                for c in range(CHUNKS):
                    cols = slice(LANES * c, LANES * c + LANES)
                    re, im = cos_sin(ref[place, w, :, cols].astype(jnp.float32))
                    re_ref[w, rows, cols] = (re * flag).astype(jnp.bfloat16)
                    im_ref[w, rows, cols] = (im * flag).astype(jnp.bfloat16)
                return marks + jnp.where(lanes == w, flag, 0.0)

            marks = lax.fori_loop(0, WIN_DEV, window, jnp.zeros((SRC, LANES), jnp.float32))
            flag_ref[rows, :] = marks.astype(jnp.bfloat16)


def receivers(one, two):
    spectrum = jax.ShapeDtypeStruct((WIN_DEV, 4 * SRC, BINS), jnp.bfloat16)
    return pl.pallas_call(
        receivers_kernel,
        out_shape=[spectrum, spectrum, jax.ShapeDtypeStruct((4 * SRC, LANES), jnp.bfloat16)],
        compiler_params=pltpu.CompilerParams(vmem_limit_bytes=32 << 20),
        cost_estimate=pl.CostEstimate(
            flops=25 * 4 * SRC * WIN_DEV * BINS, bytes_accessed=4 << 20, transcendentals=0
        ),
        name="receivers",
    )(one, two)


def correlate_kernel(
    place_ref, src_ref, re_ref, im_ref, flag_ref, table_ref, out_ref, src_sum, src_re, src_im, stacked
):
    lanes = lax.broadcasted_iota(jnp.int32, (SRC, LANES), 1)
    place = place_ref[0]
    marks = jnp.zeros((SRC, LANES), jnp.float32)
    for w in range(WIN_DEV):
        flag = src_ref[SRC * w : SRC * w + SRC, BINS:].astype(jnp.float32)
        marks = marks + jnp.where(lanes == w, flag, 0.0)
    marks = marks.astype(jnp.bfloat16)

    def prepare(c, carry):
        cols = pl.ds(pl.multiple_of(c * LANES, LANES), LANES)
        flag = src_ref[:, BINS:].astype(jnp.float32)
        re, im = cos_sin(src_ref[:, cols].astype(jnp.float32))
        re = (re * flag).astype(jnp.bfloat16).astype(jnp.float32)
        im = (im * flag).astype(jnp.bfloat16).astype(jnp.float32)
        src_re[c] = re
        src_im[c] = im
        src_sum[c] = re + im
        return carry

    lax.fori_loop(0, CHUNKS, prepare, 0)
    for d in range(4):

        def chunk(c, carry):
            cols = pl.ds(pl.multiple_of(c * LANES, LANES), LANES)
            later = pl.ds(pl.multiple_of(BINS + c * LANES, LANES), LANES)
            first, plus, minus = [], [], []
            for w in range(WIN_DEV):
                re = re_ref[w, SRC * d : SRC * d + SRC, cols].astype(jnp.float32)
                im = im_ref[w, SRC * d : SRC * d + SRC, cols].astype(jnp.float32)
                first.append(re)
                plus.append(re + im)
                minus.append(im - re)
            for s in range(SRC):
                p = q = t = None
                for w in range(WIN_DEV):
                    row = pl.ds(SRC * w + s, 1)
                    wide = (SRC, LANES)
                    both = jnp.broadcast_to(src_sum[c, row, :], wide) * first[w]
                    real = jnp.broadcast_to(src_re[c, row, :], wide) * plus[w]
                    imag = jnp.broadcast_to(src_im[c, row, :], wide) * minus[w]
                    p, q, t = (both, real, imag) if w == 0 else (p + both, q + real, t + imag)
                rows = slice(SRC * s, SRC * s + SRC)
                stacked[d, rows, cols] = (p + t).astype(jnp.bfloat16)
                stacked[d, rows, later] = (p - q).astype(jnp.bfloat16)
            return carry

        lax.fori_loop(0, CHUNKS, chunk, 0)
    for d in range(4):
        lags = jnp.dot(stacked[d], table_ref[...], preferred_element_type=jnp.float32)
        lags = lags.astype(jnp.bfloat16)
        count = lax.dot_general(
            marks,
            flag_ref[SRC * d : SRC * d + SRC, :],
            (((1,), (1,)), ((), ())),
            preferred_element_type=jnp.float32,
        )
        count = jnp.concatenate([count, jnp.zeros((SRC, LANES - SRC), jnp.float32)], 1)
        count = count.astype(jnp.bfloat16)
        to = place ^ MASKS[d]
        for w in range(N_WIN):
            out_ref[w, to, 0:32, :] = lags[32 * w : 32 * w + 32, :LANES]
            out_ref[w, to, 32:64, :] = lags[32 * w : 32 * w + 32, LANES:]
            up = 8 * (w // 4)
            out_ref[w, to, 64:PIECE_ROWS, :] = count[up : up + 8]


def correlate(place, source, rec_re, rec_im, rec_flags, table):
    vmem = pl.BlockSpec(memory_space=pltpu.VMEM)
    return pl.pallas_call(
        correlate_kernel,
        out_shape=jax.ShapeDtypeStruct((N_WIN, 4, PIECE_ROWS, LANES), jnp.bfloat16),
        in_specs=[pl.BlockSpec(memory_space=pltpu.SMEM)] + [vmem] * 5,
        out_specs=vmem,
        scratch_shapes=[pltpu.VMEM((CHUNKS, WIN_DEV * SRC, LANES), jnp.float32)] * 3
        + [pltpu.VMEM((4, SRC * SRC, 2 * BINS), jnp.bfloat16)],
        compiler_params=pltpu.CompilerParams(vmem_limit_bytes=40 << 20),
        cost_estimate=pl.CostEstimate(flops=1 << 30, bytes_accessed=4 << 20, transcendentals=0),
        name="correlate",
    )(place, source, rec_re, rec_im, rec_flags, table)


def on_device(phases, validity, plan):
    me = lax.axis_index("sta")
    place = 2 * (me // 32) + lax.rem(me, 2)
    rows = pack(phases, validity)
    own = rows.reshape(WIN_DEV, SRC, WIDTH)

    across = lax.ppermute(own, "sta", xor_pairs(32))
    pieces = lax.all_to_all(
        rows.reshape(N_Z, 8, WIDTH), "sta", 0, 0, tiled=True, axis_index_groups=ALONG_Z
    )
    pieces, across = lax.optimization_barrier((pieces, across))
    one = jnp.stack([own, across], 0)
    two = lax.ppermute(one, "sta", xor_pairs(1))
    rec_re, rec_im, rec_flags = receivers(one, two)

    owner_z = lax.rem(plan // 2, N_Z)
    held = jnp.stack(
        [lax.dynamic_index_in_dim(pieces, owner_z[k], 0, False) for k in range(STEPS)]
    )
    came = lax.all_to_all(held, "sta", 0, 0, tiled=True, axis_index_groups=QUAD)
    owner = plan[place]
    mine = lax.dynamic_slice_in_dim(came, 2 * (owner // 32) + lax.rem(owner, 2), 1, 0)
    source = lax.all_to_all(
        jnp.broadcast_to(mine, (N_Z, 8, WIDTH)),
        "sta",
        0,
        0,
        tiled=True,
        axis_index_groups=ALONG_Z,
    ).reshape(WIN_DEV * SRC, WIDTH)

    sent = correlate(place[None], source, rec_re, rec_im, rec_flags, idft_table(BINS, LAGS))
    back = lax.all_to_all(
        sent.reshape(N_WIN * 4, PIECE_ROWS, LANES),
        ("win", "sta"),
        0,
        0,
        tiled=True,
        axis_index_groups=ALL_QUADS,
    )
    total = jnp.sum(back.reshape(N_WIN, 4, PIECE_ROWS, LANES).astype(jnp.float32), 0)
    lag_sum = total[:, :64].reshape(STEPS, 2, 2, SRC, LANES).transpose(0, 2, 3, 1, 4)
    lag_sum = lag_sum.reshape(STEPS, 2, SRC, LAGS)
    first = 64 + 2 * lax.rem(lax.axis_index("win"), 4)
    pair_count = lax.dynamic_slice(total, (0, first, 0), (STEPS, 2, SRC))
    factor = 1.0 / (math.sqrt(BINS) * jnp.sqrt(jnp.maximum(pair_count, 1.0)))
    return (lag_sum * factor[..., None]).astype(jnp.bfloat16)


def solution(mesh):
    return jax.shard_map(
        on_device,
        mesh=mesh,
        in_specs=(P("win", "sta", None), P("win", "sta"), P()),
        out_specs=P(None, "win", "sta", None),
        check_vma=False,
    )
```

```python
import math

import jax
import jax.numpy as jnp
from jax import lax
from jax.experimental import pallas as pl
from jax.experimental.pallas import tpu as pltpu
from jax.sharding import PartitionSpec as P

BINS = 1024
LAGS = 256
SRC = 16
STEPS = 4
WIN_DEV = 8
N_Z = 16
N_WIN = 8
N_STA = 64
LANES = 128
CHUNKS = BINS // LANES
GROUPS = BINS // SRC
WIDTH = BINS + LANES
PIECE_ROWS = 72

QUAD = [[32 * h + 2 * z + c for h in range(2) for c in range(2)] for z in range(N_Z)]
ALONG_Z = [[32 * h + 2 * z + c for z in range(N_Z)] for h in range(2) for c in range(2)]
ALL_QUADS = [
    [w * N_STA + 32 * h + 2 * z + c for w in range(N_WIN) for h in range(2) for c in range(2)]
    for z in range(N_Z)
]
MASKS = (0, 2, 1, 3)

SINE = (
    0.7071067690849304,
    -0.029462749138474464,
    0.0003682656097225845,
    -2.1877108338230755e-06,
    7.1552790359419305e-09,
)
COSINE = (
    1.4142135381698608,
    -0.17677636444568634,
    0.003682575421407819,
    -3.061264942516573e-05,
    1.2790856374067516e-07,
)


def xor_pairs(mask):
    return [(i, i ^ mask) for i in range(N_STA)]


def idft_table(bins, lags):
    frequency = jnp.arange(bins, dtype=jnp.int32)[None, :]
    lag_offset = jnp.arange(lags, dtype=jnp.int32)[:, None] - lags // 2
    phase_turns = jnp.mod(frequency * lag_offset, 2 * bins).astype(jnp.float32)
    angles = phase_turns * (math.pi / bins)
    return jnp.concatenate([jnp.cos(angles), -jnp.sin(angles)], 1).astype(jnp.bfloat16)


def cos_sin(x):
    square = x * x
    sine, cosine = SINE[-1], COSINE[-1]
    for a, b in zip(SINE[-2::-1], COSINE[-2::-1]):
        sine = sine * square + a
        cosine = cosine * square + b
    sine = sine * x
    return 1.0 - sine * sine, sine * cosine


def flag_column(flags, first):
    lanes = lax.broadcasted_iota(jnp.int32, flags.shape, 1)
    rows = lax.broadcasted_iota(jnp.int32, flags.shape, 0)
    return jnp.sum(jnp.where(lanes == rows + first, flags, 0.0), 1, keepdims=True)


def receivers_kernel(one_ref, two_ref, *out_refs):
    matrix_refs, flag_ref = out_refs[:CHUNKS], out_refs[CHUNKS]
    lanes = lax.broadcasted_iota(jnp.int32, (LANES, LANES), 1)
    for d in range(4):
        block = (one_ref, two_ref)[d // 2]
        marks = jnp.zeros((SRC, LANES), jnp.float32)
        for w in range(WIN_DEV):
            column = flag_column(block[d % 2, w, :, BINS:].astype(jnp.float32), SRC * w)
            marks = marks + jnp.where(lanes[:SRC] == w, column, 0.0)
        flag_ref[SRC * d : SRC * d + SRC, :] = marks.astype(jnp.bfloat16)

    def window(w, carry):
        columns = []
        for d in range(4):
            block = (one_ref, two_ref)[d // 2]
            columns.append(flag_column(block[d % 2, w, :, BINS:].astype(jnp.float32), SRC * w))
        for c in range(CHUNKS):
            real, imag = [], []
            for d in range(4):
                block = (one_ref, two_ref)[d // 2]
                phase = block[d % 2, w, :, LANES * c : LANES * c + LANES].astype(jnp.float32)
                re, im = cos_sin(phase)
                real.append(re * columns[d])
                imag.append(im * columns[d])
            over = jnp.concatenate(real + [-part for part in imag], 0).T
            rows = pl.ds(pl.multiple_of(SRC * w, SRC), SRC)
            for side, values in enumerate((over,)):
                cols = slice(LANES * side, LANES * side + LANES)
                values = values.astype(jnp.bfloat16)
                for k in range(LANES // SRC):
                    matrix_refs[c][k, rows, cols] = values[SRC * k : SRC * k + SRC]
        return carry

    lax.fori_loop(0, WIN_DEV, window, 0)


def receivers(one, two):
    return pl.pallas_call(
        receivers_kernel,
        out_shape=[jax.ShapeDtypeStruct((LANES // SRC, LANES, LANES), jnp.bfloat16)] * CHUNKS
        + [jax.ShapeDtypeStruct((4 * SRC, LANES), jnp.bfloat16)],
        compiler_params=pltpu.CompilerParams(vmem_limit_bytes=12 << 20),
        cost_estimate=pl.CostEstimate(
            flops=25 * 4 * SRC * WIN_DEV * BINS, bytes_accessed=10 << 20, transcendentals=0
        ),
        name="receivers",
    )(one, two)


def correlate_kernel(
    at_ref, src_ref, flag_ref, table_ref, *refs
):
    matrix_refs, (out_ref, spectra, order, by_group, stacked) = refs[:CHUNKS], refs[CHUNKS:]
    lanes = lax.broadcasted_iota(jnp.int32, (SRC, LANES), 1)
    rows = lax.broadcasted_iota(jnp.int32, (SRC, LANES), 0)
    place = at_ref[0]
    every = src_ref[:, BINS:].astype(jnp.float32)
    at = lax.broadcasted_iota(jnp.int32, every.shape, 0) == at_ref[1]
    column = flag_column(
        jnp.broadcast_to(jnp.sum(jnp.where(at, every, 0.0), 0, keepdims=True), every.shape), 0
    )
    marks = jnp.zeros((SRC, LANES), jnp.float32)
    for w in range(WIN_DEV):
        marks = marks + jnp.where(lanes == w, column[SRC * w : SRC * w + SRC], 0.0)
    marks = marks.astype(jnp.bfloat16)

    def prepare(c, carry):
        cols = pl.ds(pl.multiple_of(c * LANES, LANES), LANES)
        re, im = cos_sin(src_ref[:, cols].astype(jnp.float32))
        for part, values in enumerate((re * column, im * column)):
            to = pl.ds(pl.multiple_of(2 * SRC * c + SRC * part, SRC), SRC)
            for w in range(WIN_DEV):
                block = values[SRC * w : SRC * w + SRC].astype(jnp.bfloat16)
                spectra[to, LANES * w : LANES * w + LANES] = block
        return carry

    lax.fori_loop(0, CHUNKS, prepare, 0)
    square = (LANES, LANES)
    column = lax.broadcasted_iota(jnp.int32, square, 1)
    for k in range(LANES // SRC):
        taken = lax.broadcasted_iota(jnp.int32, square, 0) == SRC * k + lax.rem(column, SRC)
        for w in range(WIN_DEV):
            block = jnp.where(taken & (column // SRC == w), 1.0, 0.0).astype(jnp.bfloat16)
            first = LANES * (k % 2)
            order[k // 2, LANES * w : LANES * w + LANES, first : first + LANES] = block
    for k in range(0, LANES // SRC, 2):
        ordered = jnp.dot(spectra[...], order[k // 2], preferred_element_type=jnp.float32)
        by_group[k] = ordered[:, :LANES]
        by_group[k + 1] = ordered[:, LANES:]
    same_bin = lax.rem(lanes, SRC) == rows
    low = lanes < LANES // 2

    wide = lax.broadcasted_iota(jnp.int32, (LANES, LANES), 1) < LANES // 2
    minus_low = jnp.where(wide, -1.0, 1.0).astype(jnp.bfloat16)
    minus_high = jnp.where(wide, 1.0, -1.0).astype(jnp.bfloat16)
    for chunk in range(CHUNKS):
        for k in range(LANES // SRC):
            group = chunk * (LANES // SRC) + k
            left = []
            for s in range(SRC):
                parts = []
                for part in range(2):
                    row = by_group[k, pl.ds(2 * SRC * chunk + SRC * part + s, 1), :]
                    row = jnp.broadcast_to(row, (SRC, LANES))
                    parts.append(jnp.where(same_bin, row, 0.0).astype(jnp.bfloat16))
                left.append(jnp.concatenate(parts, 1))
            left = jnp.concatenate(left, 0)
            upper = matrix_refs[chunk][k]
            turned = jnp.concatenate([upper[:, LANES // 2 :], upper[:, : LANES // 2]], 1)
            lower = [turned * minus_low, upper * minus_high]
            right = [jnp.concatenate([upper, turned], 1), jnp.concatenate(lower, 1)]
            right = jnp.concatenate(right, 0)
            found = jnp.dot(left, right, preferred_element_type=jnp.float32)
            real = slice(SRC * group, SRC * group + SRC)
            imag = slice(BINS + SRC * group, BINS + SRC * group + SRC)
            for w in range(N_WIN):
                even = found[2 * SRC * w : 2 * SRC * w + SRC]
                odd = found[2 * SRC * w + SRC : 2 * SRC * w + 2 * SRC]
                cols = slice(LANES * w, LANES * w + LANES)
                stacked[real, cols] = jnp.where(low, even[:, :LANES], odd[:, LANES:]).astype(
                    jnp.bfloat16
                )
                stacked[imag, cols] = jnp.where(low, even[:, LANES:], odd[:, :LANES]).astype(
                    jnp.bfloat16
                )
    counts = []
    for d in range(4):
        count = lax.dot_general(
            marks,
            flag_ref[SRC * d : SRC * d + SRC, :],
            (((1,), (1,)), ((), ())),
            preferred_element_type=jnp.float32,
        )
        count = jnp.concatenate([count, jnp.zeros((SRC, LANES - SRC), jnp.float32)], 1)
        counts.append(count.astype(jnp.bfloat16))
    for pair in range(0, N_WIN, 2):
        cols = slice(LANES * pair, LANES * pair + 2 * LANES)
        lags = jnp.dot(table_ref[...], stacked[:, cols], preferred_element_type=jnp.float32)
        for w in range(pair, pair + 2):
            first = LANES * (w - pair)
            turned = lags[:, first : first + LANES].T.astype(jnp.bfloat16)
            for d in range(4):
                to = place ^ MASKS[d]
                for s in range(2):
                    part = turned[4 * SRC * s + SRC * d : 4 * SRC * s + SRC * d + SRC]
                    out_ref[w, to, SRC * s : SRC * s + SRC, :] = part[:, :LANES]
                    out_ref[w, to, 2 * SRC + SRC * s : 3 * SRC + SRC * s, :] = part[:, LANES:]
                up = 8 * (w // 4)
                out_ref[w, to, 64:PIECE_ROWS, :] = counts[d][up : up + 8]


def correlate(at, source, matrices, rec_flags, table):
    vmem = pl.BlockSpec(memory_space=pltpu.VMEM)
    return pl.pallas_call(
        correlate_kernel,
        out_shape=jax.ShapeDtypeStruct((N_WIN, 4, PIECE_ROWS, LANES), jnp.bfloat16),
        in_specs=[pl.BlockSpec(memory_space=pltpu.SMEM)] + [vmem] * (3 + CHUNKS),
        out_specs=vmem,
        scratch_shapes=[
            pltpu.VMEM((2 * SRC * CHUNKS, BINS), jnp.bfloat16),
            pltpu.VMEM((LANES // SRC // 2, BINS, 2 * LANES), jnp.bfloat16),
            pltpu.VMEM((LANES // SRC, 2 * SRC * CHUNKS, LANES), jnp.float32),
            pltpu.VMEM((2 * BINS, SRC * 4 * SRC), jnp.bfloat16),
        ],
        compiler_params=pltpu.CompilerParams(vmem_limit_bytes=20 << 20),
        cost_estimate=pl.CostEstimate(flops=1 << 30, bytes_accessed=12 << 20, transcendentals=0),
        name="correlate",
    )(at, source, rec_flags, table, *matrices)


def on_device(phases, validity, plan):
    me = lax.axis_index("sta")
    place = 2 * (me // 32) + lax.rem(me, 2)
    pieces = lax.all_to_all(
        phases.reshape(N_Z, 8, BINS), "sta", 0, 0, tiled=True, axis_index_groups=ALONG_Z
    )

    flags = validity.astype(jnp.bfloat16).reshape(1, 1, LANES)
    own = jnp.concatenate([phases, jnp.broadcast_to(flags, (WIN_DEV, SRC, LANES))], -1)
    across = lax.ppermute(own, "sta", xor_pairs(32))
    pieces, across = lax.optimization_barrier((pieces, across))
    one = jnp.stack([own, across], 0)
    two = lax.ppermute(one, "sta", xor_pairs(1))
    *matrices, rec_flags = receivers(one, two)

    owner_z = lax.rem(plan // 2, N_Z)
    held = jnp.stack(
        [lax.dynamic_index_in_dim(pieces, owner_z[k], 0, False) for k in range(STEPS)]
    )
    held = jnp.concatenate([held, jnp.broadcast_to(flags, (STEPS, 8, LANES))], -1)
    came = lax.all_to_all(held, "sta", 0, 0, tiled=True, axis_index_groups=QUAD)
    owner = plan[place]
    owner_place = 2 * (owner // 32) + lax.rem(owner, 2)
    mine = lax.dynamic_index_in_dim(came, owner_place, 0, False)[:, :BINS]
    quad_flags = came[:, :2, BINS:].reshape(8, LANES)
    sent = jnp.concatenate([mine, quad_flags], 1)
    source = lax.all_to_all(
        jnp.broadcast_to(sent[None], (N_Z, 8, WIDTH)),
        "sta",
        0,
        0,
        tiled=True,
        axis_index_groups=ALONG_Z,
    ).reshape(WIN_DEV * SRC, WIDTH)
    flag_row = 8 * lax.rem(owner // 2, N_Z) + 2 * owner_place

    sent = correlate(
        jnp.stack([place, flag_row]), source, matrices, rec_flags, idft_table(BINS, LAGS)
    )
    back = lax.all_to_all(
        sent.reshape(N_WIN * 4, PIECE_ROWS, LANES),
        ("win", "sta"),
        0,
        0,
        tiled=True,
        axis_index_groups=ALL_QUADS,
    )
    total = jnp.sum(back.reshape(N_WIN, 4, PIECE_ROWS, LANES).astype(jnp.float32), 0)
    lag_sum = total[:, :64].reshape(STEPS, 2, 2, SRC, LANES).transpose(0, 2, 3, 1, 4)
    lag_sum = lag_sum.reshape(STEPS, 2, SRC, LAGS)
    first = 64 + 2 * lax.rem(lax.axis_index("win"), 4)
    pair_count = lax.dynamic_slice(total, (0, first, 0), (STEPS, 2, SRC))
    factor = 1.0 / (math.sqrt(BINS) * jnp.sqrt(jnp.maximum(pair_count, 1.0)))
    return (lag_sum * factor[..., None]).astype(jnp.bfloat16)


def solution(mesh):
    return jax.shard_map(
        on_device,
        mesh=mesh,
        in_specs=(P("win", "sta", None), P("win", "sta"), P()),
        out_specs=P(None, "win", "sta", None),
        check_vma=False,
    )
```

```python
import math

import jax
import jax.numpy as jnp
from jax import lax
from jax.experimental import pallas as pl
from jax.experimental.pallas import tpu as pltpu
from jax.sharding import PartitionSpec as P

BINS = 1024
LAGS = 256
SRC = 16
STEPS = 4
WIN_DEV = 8
N_Z = 16
N_WIN = 8
N_STA = 64
LANES = 128
CHUNKS = BINS // LANES
GROUPS = BINS // SRC
WIDTH = BINS + LANES
PIECE_ROWS = 72

QUAD = [[32 * h + 2 * z + c for h in range(2) for c in range(2)] for z in range(N_Z)]
ALONG_Z = [[32 * h + 2 * z + c for z in range(N_Z)] for h in range(2) for c in range(2)]
ALL_QUADS = [
    [w * N_STA + 32 * h + 2 * z + c for w in range(N_WIN) for h in range(2) for c in range(2)]
    for z in range(N_Z)
]
MASKS = (0, 2, 1, 3)

SINE = (
    0.7071067690849304,
    -0.029462749138474464,
    0.0003682656097225845,
    -2.1877108338230755e-06,
    7.1552790359419305e-09,
)
COSINE = (
    1.4142135381698608,
    -0.17677636444568634,
    0.003682575421407819,
    -3.061264942516573e-05,
    1.2790856374067516e-07,
)


def xor_pairs(mask):
    return [(i, i ^ mask) for i in range(N_STA)]


def idft_table(bins, lags):
    frequency = jnp.arange(bins, dtype=jnp.int32)[None, :]
    lag_offset = jnp.arange(lags, dtype=jnp.int32)[:, None] - lags // 2
    phase_turns = jnp.mod(frequency * lag_offset, 2 * bins).astype(jnp.float32)
    angles = phase_turns * (math.pi / bins)
    return jnp.concatenate([jnp.cos(angles), -jnp.sin(angles)], 1).astype(jnp.bfloat16)


def cos_sin(x):
    square = x * x
    sine, cosine = SINE[-1], COSINE[-1]
    for a, b in zip(SINE[-2::-1], COSINE[-2::-1]):
        sine = sine * square + a
        cosine = cosine * square + b
    sine = sine * x
    return 1.0 - sine * sine, sine * cosine


def flag_column(flags, first):
    lanes = lax.broadcasted_iota(jnp.int32, flags.shape, 1)
    rows = lax.broadcasted_iota(jnp.int32, flags.shape, 0)
    return jnp.sum(jnp.where(lanes == rows + first, flags, 0.0), 1, keepdims=True)


def receivers_kernel(one_ref, two_ref, *out_refs):
    matrix_refs, flag_ref = out_refs[:CHUNKS], out_refs[CHUNKS]
    lanes = lax.broadcasted_iota(jnp.int32, (LANES, LANES), 1)
    for d in range(4):
        block = (one_ref, two_ref)[d // 2]
        marks = jnp.zeros((SRC, LANES), jnp.float32)
        for w in range(WIN_DEV):
            column = flag_column(block[d % 2, w, :, BINS:].astype(jnp.float32), SRC * w)
            marks = marks + jnp.where(lanes[:SRC] == w, column, 0.0)
        flag_ref[SRC * d : SRC * d + SRC, :] = marks.astype(jnp.bfloat16)

    def window(w, carry):
        columns = []
        for d in range(4):
            block = (one_ref, two_ref)[d // 2]
            columns.append(flag_column(block[d % 2, w, :, BINS:].astype(jnp.float32), SRC * w))
        for c in range(CHUNKS):
            real, imag = [], []
            for d in range(4):
                block = (one_ref, two_ref)[d // 2]
                phase = block[d % 2, w, :, LANES * c : LANES * c + LANES].astype(jnp.float32)
                re, im = cos_sin(phase)
                real.append(re * columns[d])
                imag.append(im * columns[d])
            over = jnp.concatenate(real + [-part for part in imag], 0).T
            rows = pl.ds(pl.multiple_of(SRC * w, SRC), SRC)
            for side, values in enumerate((over,)):
                cols = slice(LANES * side, LANES * side + LANES)
                values = values.astype(jnp.bfloat16)
                for k in range(LANES // SRC):
                    matrix_refs[c][k, rows, cols] = values[SRC * k : SRC * k + SRC]
        return carry

    lax.fori_loop(0, WIN_DEV, window, 0)


def receivers(one, two):
    return pl.pallas_call(
        receivers_kernel,
        out_shape=[jax.ShapeDtypeStruct((LANES // SRC, LANES, LANES), jnp.bfloat16)] * CHUNKS
        + [jax.ShapeDtypeStruct((4 * SRC, LANES), jnp.bfloat16)],
        compiler_params=pltpu.CompilerParams(vmem_limit_bytes=12 << 20),
        cost_estimate=pl.CostEstimate(
            flops=25 * 4 * SRC * WIN_DEV * BINS, bytes_accessed=10 << 20, transcendentals=0
        ),
        name="receivers",
    )(one, two)


def correlate_kernel(
    at_ref, src_ref, flag_ref, table_ref, *refs
):
    matrix_refs, (out_ref, spectra, order, by_group, stacked) = refs[:CHUNKS], refs[CHUNKS:]
    lanes = lax.broadcasted_iota(jnp.int32, (SRC, LANES), 1)
    rows = lax.broadcasted_iota(jnp.int32, (SRC, LANES), 0)
    place = at_ref[0]
    every = src_ref[:, BINS:].astype(jnp.float32)
    at = lax.broadcasted_iota(jnp.int32, every.shape, 0) == at_ref[1]
    column = flag_column(
        jnp.broadcast_to(jnp.sum(jnp.where(at, every, 0.0), 0, keepdims=True), every.shape), 0
    )
    marks = jnp.zeros((SRC, LANES), jnp.float32)
    for w in range(WIN_DEV):
        marks = marks + jnp.where(lanes == w, column[SRC * w : SRC * w + SRC], 0.0)
    marks = marks.astype(jnp.bfloat16)

    def prepare(c, carry):
        cols = slice(c * LANES, c * LANES + LANES)
        re, im = cos_sin(src_ref[:, cols].astype(jnp.float32))
        for part, values in enumerate((re * column, im * column)):
            to = slice(2 * SRC * c + SRC * part, 2 * SRC * c + SRC * part + SRC)
            for w in range(WIN_DEV):
                block = values[SRC * w : SRC * w + SRC].astype(jnp.bfloat16)
                spectra[to, LANES * w : LANES * w + LANES] = block
        return carry

    for c in range(CHUNKS):
        prepare(c, 0)
    square = (LANES, LANES)
    column = lax.broadcasted_iota(jnp.int32, square, 1)
    for k in range(LANES // SRC):
        taken = lax.broadcasted_iota(jnp.int32, square, 0) == SRC * k + lax.rem(column, SRC)
        for w in range(WIN_DEV):
            block = jnp.where(taken & (column // SRC == w), 1.0, 0.0).astype(jnp.bfloat16)
            first = LANES * (k % 2)
            order[k // 2, LANES * w : LANES * w + LANES, first : first + LANES] = block
    for k in range(0, LANES // SRC, 2):
        ordered = jnp.dot(spectra[...], order[k // 2], preferred_element_type=jnp.float32)
        by_group[k] = ordered[:, :LANES]
        by_group[k + 1] = ordered[:, LANES:]
    same_bin = lax.rem(lanes, SRC) == rows
    low = lanes < LANES // 2

    wide = lax.broadcasted_iota(jnp.int32, (LANES, LANES), 1) < LANES // 2
    minus_low = jnp.where(wide, -1.0, 1.0).astype(jnp.bfloat16)
    minus_high = jnp.where(wide, 1.0, -1.0).astype(jnp.bfloat16)
    for chunk in range(CHUNKS):
        for k in range(LANES // SRC):
            group = chunk * (LANES // SRC) + k
            left = []
            for s in range(SRC):
                parts = []
                for part in range(2):
                    row = by_group[k, pl.ds(2 * SRC * chunk + SRC * part + s, 1), :]
                    row = jnp.broadcast_to(row, (SRC, LANES))
                    parts.append(jnp.where(same_bin, row, 0.0).astype(jnp.bfloat16))
                left.append(jnp.concatenate(parts, 1))
            left = jnp.concatenate(left, 0)
            upper = matrix_refs[chunk][k]
            turned = jnp.concatenate([upper[:, LANES // 2 :], upper[:, : LANES // 2]], 1)
            lower = [turned * minus_low, upper * minus_high]
            right = [jnp.concatenate([upper, turned], 1), jnp.concatenate(lower, 1)]
            right = jnp.concatenate(right, 0)
            found = jnp.dot(left, right, preferred_element_type=jnp.float32)
            real = slice(SRC * group, SRC * group + SRC)
            imag = slice(BINS + SRC * group, BINS + SRC * group + SRC)
            for w in range(N_WIN):
                even = found[2 * SRC * w : 2 * SRC * w + SRC]
                odd = found[2 * SRC * w + SRC : 2 * SRC * w + 2 * SRC]
                cols = slice(LANES * w, LANES * w + LANES)
                stacked[real, cols] = jnp.where(low, even[:, :LANES], odd[:, LANES:]).astype(
                    jnp.bfloat16
                )
                stacked[imag, cols] = jnp.where(low, even[:, LANES:], odd[:, :LANES]).astype(
                    jnp.bfloat16
                )
    counts = []
    for d in range(4):
        count = lax.dot_general(
            marks,
            flag_ref[SRC * d : SRC * d + SRC, :],
            (((1,), (1,)), ((), ())),
            preferred_element_type=jnp.float32,
        )
        counts.append(jnp.concatenate([count, jnp.zeros((SRC, LANES - SRC), jnp.float32)], 1))
    for pair in range(0, N_WIN, 2):
        cols = slice(LANES * pair, LANES * pair + 2 * LANES)
        lags = jnp.dot(table_ref[...], stacked[:, cols], preferred_element_type=jnp.float32)
        for w in range(pair, pair + 2):
            first = LANES * (w - pair)
            turned = lags[:, first : first + LANES].T.astype(jnp.bfloat16)
            for d in range(4):
                to = place ^ MASKS[d]
                for s in range(2):
                    part = turned[4 * SRC * s + SRC * d : 4 * SRC * s + SRC * d + SRC]
                    out_ref[w, to, SRC * s : SRC * s + SRC, :] = part[:, :LANES]
                    out_ref[w, to, 2 * SRC + SRC * s : 3 * SRC + SRC * s, :] = part[:, LANES:]
                pair_counts = [counts[d][2 * w : 2 * w + 2], jnp.zeros((6, LANES), jnp.float32)]
                pair_counts = jnp.concatenate(pair_counts, 0).astype(jnp.bfloat16)
                out_ref[w, to, 64:PIECE_ROWS, :] = pair_counts


def correlate(at, source, matrices, rec_flags, table):
    vmem = pl.BlockSpec(memory_space=pltpu.VMEM)
    return pl.pallas_call(
        correlate_kernel,
        out_shape=jax.ShapeDtypeStruct((N_WIN, 4, PIECE_ROWS, LANES), jnp.bfloat16),
        in_specs=[pl.BlockSpec(memory_space=pltpu.SMEM)] + [vmem] * (3 + CHUNKS),
        out_specs=vmem,
        scratch_shapes=[
            pltpu.VMEM((2 * SRC * CHUNKS, BINS), jnp.bfloat16),
            pltpu.VMEM((LANES // SRC // 2, BINS, 2 * LANES), jnp.bfloat16),
            pltpu.VMEM((LANES // SRC, 2 * SRC * CHUNKS, LANES), jnp.float32),
            pltpu.VMEM((2 * BINS, SRC * 4 * SRC), jnp.bfloat16),
        ],
        compiler_params=pltpu.CompilerParams(vmem_limit_bytes=20 << 20),
        cost_estimate=pl.CostEstimate(flops=1 << 30, bytes_accessed=12 << 20, transcendentals=0),
        name="correlate",
    )(at, source, rec_flags, table, *matrices)


def on_device(phases, validity, plan):
    me = lax.axis_index("sta")
    place = 2 * (me // 32) + lax.rem(me, 2)
    pieces = lax.all_to_all(
        phases.reshape(N_Z, 8, BINS), "sta", 0, 0, tiled=True, axis_index_groups=ALONG_Z
    )

    flags = validity.astype(jnp.bfloat16).reshape(1, 1, LANES)
    own = jnp.concatenate([phases, jnp.broadcast_to(flags, (WIN_DEV, SRC, LANES))], -1)
    across = lax.ppermute(own, "sta", xor_pairs(32))
    pieces, across = lax.optimization_barrier((pieces, across))
    one = jnp.stack([own, across], 0)
    two = lax.ppermute(one, "sta", xor_pairs(1))
    *matrices, rec_flags = receivers(one, two)

    owner_z = lax.rem(plan // 2, N_Z)
    held = jnp.stack(
        [lax.dynamic_index_in_dim(pieces, owner_z[k], 0, False) for k in range(STEPS)]
    )
    held = jnp.concatenate([held, jnp.broadcast_to(flags, (STEPS, 8, LANES))], -1)
    came = lax.all_to_all(held, "sta", 0, 0, tiled=True, axis_index_groups=QUAD)
    owner = plan[place]
    owner_place = 2 * (owner // 32) + lax.rem(owner, 2)
    mine = lax.dynamic_index_in_dim(came, owner_place, 0, False)[:, :BINS]
    quad_flags = came[:, :2, BINS:].reshape(8, LANES)
    sent = jnp.concatenate([mine, quad_flags], 1)
    source = lax.all_to_all(
        jnp.broadcast_to(sent[None], (N_Z, 8, WIDTH)),
        "sta",
        0,
        0,
        tiled=True,
        axis_index_groups=ALONG_Z,
    ).reshape(WIN_DEV * SRC, WIDTH)
    flag_row = 8 * lax.rem(owner // 2, N_Z) + 2 * owner_place

    sent = correlate(
        jnp.stack([place, flag_row]), source, matrices, rec_flags, idft_table(BINS, LAGS)
    )
    back = lax.all_to_all(
        sent.reshape(N_WIN * 4, PIECE_ROWS, LANES),
        ("win", "sta"),
        0,
        0,
        tiled=True,
        axis_index_groups=ALL_QUADS,
    )
    total = jnp.sum(back.reshape(N_WIN, 4, PIECE_ROWS, LANES).astype(jnp.float32), 0)
    lag_sum = total[:, :64].reshape(STEPS, 2, 2, SRC, LANES).transpose(0, 2, 3, 1, 4)
    lag_sum = lag_sum.reshape(STEPS, 2, SRC, LAGS)
    pair_count = total[:, 64:66, :SRC]
    factor = 1.0 / (math.sqrt(BINS) * jnp.sqrt(jnp.maximum(pair_count, 1.0)))
    return (lag_sum * factor[..., None]).astype(jnp.bfloat16)


def solution(mesh):
    return jax.shard_map(
        on_device,
        mesh=mesh,
        in_specs=(P("win", "sta", None), P("win", "sta"), P()),
        out_specs=P(None, "win", "sta", None),
        check_vma=False,
    )
```

```python
import math

import jax
import jax.numpy as jnp
from jax import lax
from jax.experimental import pallas as pl
from jax.experimental.pallas import tpu as pltpu
from jax.sharding import PartitionSpec as P

BINS = 1024
LAGS = 256
SRC = 16
STEPS = 4
WIN_DEV = 8
N_Z = 16
N_WIN = 8
N_STA = 64
LANES = 128
CHUNKS = BINS // LANES
GROUPS = BINS // SRC
WIDTH = BINS + LANES
PIECE_ROWS = 72

QUAD = [[32 * h + 2 * z + c for h in range(2) for c in range(2)] for z in range(N_Z)]
ALONG_Z = [[32 * h + 2 * z + c for z in range(N_Z)] for h in range(2) for c in range(2)]
ALL_QUADS = [
    [w * N_STA + 32 * h + 2 * z + c for w in range(N_WIN) for h in range(2) for c in range(2)]
    for z in range(N_Z)
]
MASKS = (0, 2, 1, 3)

SINE = (
    0.7071067690849304,
    -0.029462749138474464,
    0.0003682656097225845,
    -2.1877108338230755e-06,
    7.1552790359419305e-09,
)
COSINE = (
    1.4142135381698608,
    -0.17677636444568634,
    0.003682575421407819,
    -3.061264942516573e-05,
    1.2790856374067516e-07,
)


def xor_pairs(mask):
    return [(i, i ^ mask) for i in range(N_STA)]


def idft_table(bins, lags):
    frequency = jnp.arange(bins, dtype=jnp.int32)[None, :]
    lag_offset = jnp.arange(lags, dtype=jnp.int32)[:, None] - lags // 2
    phase_turns = jnp.mod(frequency * lag_offset, 2 * bins).astype(jnp.float32)
    angles = phase_turns * (math.pi / bins)
    return jnp.concatenate([jnp.cos(angles), -jnp.sin(angles)], 1).astype(jnp.bfloat16)


def cos_sin(x):
    square = x * x
    sine, cosine = SINE[-1], COSINE[-1]
    for a, b in zip(SINE[-2::-1], COSINE[-2::-1]):
        sine = sine * square + a
        cosine = cosine * square + b
    sine = sine * x
    return 1.0 - sine * sine, sine * cosine


def flag_column(flags, first):
    lanes = lax.broadcasted_iota(jnp.int32, flags.shape, 1)
    rows = lax.broadcasted_iota(jnp.int32, flags.shape, 0)
    return jnp.sum(jnp.where(lanes == rows + first, flags, 0.0), 1, keepdims=True)


def receivers_kernel(one_ref, two_ref, *out_refs):
    matrix_refs, flag_ref = out_refs[:CHUNKS], out_refs[CHUNKS]
    lanes = lax.broadcasted_iota(jnp.int32, (LANES, LANES), 1)
    for d in range(4):
        block = (one_ref, two_ref)[d // 2]
        marks = jnp.zeros((SRC, LANES), jnp.float32)
        for w in range(WIN_DEV):
            column = flag_column(block[d % 2, w, :, BINS:].astype(jnp.float32), SRC * w)
            marks = marks + jnp.where(lanes[:SRC] == w, column, 0.0)
        flag_ref[SRC * d : SRC * d + SRC, :] = marks.astype(jnp.bfloat16)

    def window(w, carry):
        columns = []
        for d in range(4):
            block = (one_ref, two_ref)[d // 2]
            columns.append(flag_column(block[d % 2, w, :, BINS:].astype(jnp.float32), SRC * w))
        for c in range(CHUNKS):
            real, imag = [], []
            for d in range(4):
                block = (one_ref, two_ref)[d // 2]
                phase = block[d % 2, w, :, LANES * c : LANES * c + LANES].astype(jnp.float32)
                re, im = cos_sin(phase)
                real.append(re * columns[d])
                imag.append(im * columns[d])
            over = jnp.concatenate(real + [-part for part in imag], 0).T
            rows = pl.ds(pl.multiple_of(SRC * w, SRC), SRC)
            for side, values in enumerate((over,)):
                cols = slice(LANES * side, LANES * side + LANES)
                values = values.astype(jnp.bfloat16)
                for k in range(LANES // SRC):
                    matrix_refs[c][k, rows, cols] = values[SRC * k : SRC * k + SRC]
        return carry

    lax.fori_loop(0, WIN_DEV, window, 0)


def receivers(one, two):
    return pl.pallas_call(
        receivers_kernel,
        out_shape=[jax.ShapeDtypeStruct((LANES // SRC, LANES, LANES), jnp.bfloat16)] * CHUNKS
        + [jax.ShapeDtypeStruct((4 * SRC, LANES), jnp.bfloat16)],
        compiler_params=pltpu.CompilerParams(vmem_limit_bytes=12 << 20),
        cost_estimate=pl.CostEstimate(
            flops=25 * 4 * SRC * WIN_DEV * BINS, bytes_accessed=10 << 20, transcendentals=0
        ),
        name="receivers",
    )(one, two)


def correlate_kernel(
    at_ref, src_ref, flag_ref, table_ref, *refs
):
    matrix_refs, (out_ref, by_group, stacked) = refs[:CHUNKS], refs[CHUNKS:]
    lanes = lax.broadcasted_iota(jnp.int32, (SRC, LANES), 1)
    rows = lax.broadcasted_iota(jnp.int32, (SRC, LANES), 0)
    place = at_ref[0]
    every = src_ref[:, BINS:].astype(jnp.float32)
    at = lax.broadcasted_iota(jnp.int32, every.shape, 0) == at_ref[1]
    column = flag_column(
        jnp.broadcast_to(jnp.sum(jnp.where(at, every, 0.0), 0, keepdims=True), every.shape), 0
    )
    marks = jnp.zeros((SRC, LANES), jnp.float32)
    for w in range(WIN_DEV):
        marks = marks + jnp.where(lanes == w, column[SRC * w : SRC * w + SRC], 0.0)
    marks = marks.astype(jnp.bfloat16)

    def prepare(c, carry):
        cols = slice(c * LANES, c * LANES + LANES)
        re, im = cos_sin(src_ref[:, cols].astype(jnp.float32))
        for part, values in enumerate((re * column, im * column)):
            to = slice(2 * SRC * c + SRC * part, 2 * SRC * c + SRC * part + SRC)
            for k in range(LANES // SRC):
                found = None
                for w in range(WIN_DEV):
                    block = values[SRC * w : SRC * w + SRC]
                    shift = SRC * ((w - k) % WIN_DEV)
                    block = pltpu.roll(block, shift, 1) if shift else block
                    found = block if found is None else jnp.where(lanes // SRC == w, block, found)
                by_group[k, to, :] = found
        return carry

    for c in range(CHUNKS):
        prepare(c, 0)
    same_bin = lax.rem(lanes, SRC) == rows
    low = lanes < LANES // 2

    wide = lax.broadcasted_iota(jnp.int32, (LANES, LANES), 1) < LANES // 2
    minus_low = jnp.where(wide, -1.0, 1.0).astype(jnp.bfloat16)
    minus_high = jnp.where(wide, 1.0, -1.0).astype(jnp.bfloat16)
    for chunk in range(CHUNKS):
        for k in range(LANES // SRC):
            group = chunk * (LANES // SRC) + k
            left = []
            for s in range(SRC):
                parts = []
                for part in range(2):
                    row = by_group[k, pl.ds(2 * SRC * chunk + SRC * part + s, 1), :]
                    row = jnp.broadcast_to(row, (SRC, LANES))
                    parts.append(jnp.where(same_bin, row, 0.0).astype(jnp.bfloat16))
                left.append(jnp.concatenate(parts, 1))
            left = jnp.concatenate(left, 0)
            upper = matrix_refs[chunk][k]
            turned = jnp.concatenate([upper[:, LANES // 2 :], upper[:, : LANES // 2]], 1)
            lower = [turned * minus_low, upper * minus_high]
            right = [jnp.concatenate([upper, turned], 1), jnp.concatenate(lower, 1)]
            right = jnp.concatenate(right, 0)
            found = jnp.dot(left, right, preferred_element_type=jnp.float32)
            real = slice(SRC * group, SRC * group + SRC)
            imag = slice(BINS + SRC * group, BINS + SRC * group + SRC)
            for w in range(N_WIN):
                even = found[2 * SRC * w : 2 * SRC * w + SRC]
                odd = found[2 * SRC * w + SRC : 2 * SRC * w + 2 * SRC]
                cols = slice(LANES * w, LANES * w + LANES)
                stacked[real, cols] = jnp.where(low, even[:, :LANES], odd[:, LANES:]).astype(
                    jnp.bfloat16
                )
                stacked[imag, cols] = jnp.where(low, even[:, LANES:], odd[:, :LANES]).astype(
                    jnp.bfloat16
                )
    counts = []
    for d in range(4):
        count = lax.dot_general(
            marks,
            flag_ref[SRC * d : SRC * d + SRC, :],
            (((1,), (1,)), ((), ())),
            preferred_element_type=jnp.float32,
        )
        counts.append(jnp.concatenate([count, jnp.zeros((SRC, LANES - SRC), jnp.float32)], 1))
    for pair in range(0, N_WIN, 2):
        cols = slice(LANES * pair, LANES * pair + 2 * LANES)
        lags = jnp.dot(table_ref[...], stacked[:, cols], preferred_element_type=jnp.float32)
        for w in range(pair, pair + 2):
            first = LANES * (w - pair)
            turned = lags[:, first : first + LANES].T.astype(jnp.bfloat16)
            for d in range(4):
                to = place ^ MASKS[d]
                for s in range(2):
                    part = turned[4 * SRC * s + SRC * d : 4 * SRC * s + SRC * d + SRC]
                    out_ref[w, to, SRC * s : SRC * s + SRC, :] = part[:, :LANES]
                    out_ref[w, to, 2 * SRC + SRC * s : 3 * SRC + SRC * s, :] = part[:, LANES:]
                pair_counts = [counts[d][2 * w : 2 * w + 2], jnp.zeros((6, LANES), jnp.float32)]
                pair_counts = jnp.concatenate(pair_counts, 0).astype(jnp.bfloat16)
                out_ref[w, to, 64:PIECE_ROWS, :] = pair_counts


def correlate(at, source, matrices, rec_flags, table):
    vmem = pl.BlockSpec(memory_space=pltpu.VMEM)
    return pl.pallas_call(
        correlate_kernel,
        out_shape=jax.ShapeDtypeStruct((N_WIN, 4, PIECE_ROWS, LANES), jnp.bfloat16),
        in_specs=[pl.BlockSpec(memory_space=pltpu.SMEM)] + [vmem] * (3 + CHUNKS),
        out_specs=vmem,
        scratch_shapes=[
            pltpu.VMEM((LANES // SRC, 2 * SRC * CHUNKS, LANES), jnp.float32),
            pltpu.VMEM((2 * BINS, SRC * 4 * SRC), jnp.bfloat16),
        ],
        compiler_params=pltpu.CompilerParams(vmem_limit_bytes=20 << 20),
        cost_estimate=pl.CostEstimate(flops=1 << 30, bytes_accessed=12 << 20, transcendentals=0),
        name="correlate",
    )(at, source, rec_flags, table, *matrices)


def on_device(phases, validity, plan):
    me = lax.axis_index("sta")
    place = 2 * (me // 32) + lax.rem(me, 2)
    pieces = lax.all_to_all(
        phases.reshape(N_Z, 8, BINS), "sta", 0, 0, tiled=True, axis_index_groups=ALONG_Z
    )

    flags = validity.astype(jnp.bfloat16).reshape(1, 1, LANES)
    own = jnp.concatenate([phases, jnp.broadcast_to(flags, (WIN_DEV, SRC, LANES))], -1)
    across = lax.ppermute(own, "sta", xor_pairs(32))
    pieces, across = lax.optimization_barrier((pieces, across))
    one = jnp.stack([own, across], 0)
    two = lax.ppermute(one, "sta", xor_pairs(1))
    *matrices, rec_flags = receivers(one, two)

    owner_z = lax.rem(plan // 2, N_Z)
    held = jnp.stack(
        [lax.dynamic_index_in_dim(pieces, owner_z[k], 0, False) for k in range(STEPS)]
    )
    held = jnp.concatenate([held, jnp.broadcast_to(flags, (STEPS, 8, LANES))], -1)
    came = lax.all_to_all(held, "sta", 0, 0, tiled=True, axis_index_groups=QUAD)
    owner = plan[place]
    owner_place = 2 * (owner // 32) + lax.rem(owner, 2)
    mine = lax.dynamic_index_in_dim(came, owner_place, 0, False)[:, :BINS]
    quad_flags = came[:, :2, BINS:].reshape(8, LANES)
    sent = jnp.concatenate([mine, quad_flags], 1)
    source = lax.all_to_all(
        jnp.broadcast_to(sent[None], (N_Z, 8, WIDTH)),
        "sta",
        0,
        0,
        tiled=True,
        axis_index_groups=ALONG_Z,
    ).reshape(WIN_DEV * SRC, WIDTH)
    flag_row = 8 * lax.rem(owner // 2, N_Z) + 2 * owner_place

    sent = correlate(
        jnp.stack([place, flag_row]), source, matrices, rec_flags, idft_table(BINS, LAGS)
    )
    back = lax.all_to_all(
        sent.reshape(N_WIN * 4, PIECE_ROWS, LANES),
        ("win", "sta"),
        0,
        0,
        tiled=True,
        axis_index_groups=ALL_QUADS,
    )
    total = jnp.sum(back.reshape(N_WIN, 4, PIECE_ROWS, LANES).astype(jnp.float32), 0)
    lag_sum = total[:, :64].reshape(STEPS, 2, 2, SRC, LANES).transpose(0, 2, 3, 1, 4)
    lag_sum = lag_sum.reshape(STEPS, 2, SRC, LAGS)
    pair_count = total[:, 64:66, :SRC]
    factor = 1.0 / (math.sqrt(BINS) * jnp.sqrt(jnp.maximum(pair_count, 1.0)))
    return (lag_sum * factor[..., None]).astype(jnp.bfloat16)


def solution(mesh):
    return jax.shard_map(
        on_device,
        mesh=mesh,
        in_specs=(P("win", "sta", None), P("win", "sta"), P()),
        out_specs=P(None, "win", "sta", None),
        check_vma=False,
    )
```

```python
import math

import jax
import jax.numpy as jnp
from jax import lax
from jax.experimental import pallas as pl
from jax.experimental.pallas import tpu as pltpu
from jax.sharding import PartitionSpec as P

BINS = 1024
LAGS = 256
SRC = 16
STEPS = 4
WIN_DEV = 8
N_Z = 16
N_WIN = 8
N_STA = 64
LANES = 128
CHUNKS = BINS // LANES
GROUPS = BINS // SRC
WIDTH = BINS + LANES
PIECE_ROWS = 72

QUAD = [[32 * h + 2 * z + c for h in range(2) for c in range(2)] for z in range(N_Z)]
ALONG_Z = [[32 * h + 2 * z + c for z in range(N_Z)] for h in range(2) for c in range(2)]
ALL_QUADS = [
    [w * N_STA + 32 * h + 2 * z + c for w in range(N_WIN) for h in range(2) for c in range(2)]
    for z in range(N_Z)
]
MASKS = (0, 2, 1, 3)

SINE = (
    0.7071067690849304,
    -0.029462749138474464,
    0.0003682656097225845,
    -2.1877108338230755e-06,
    7.1552790359419305e-09,
)
COSINE = (
    1.4142135381698608,
    -0.17677636444568634,
    0.003682575421407819,
    -3.061264942516573e-05,
    1.2790856374067516e-07,
)


def xor_pairs(mask):
    return [(i, i ^ mask) for i in range(N_STA)]


def idft_table(bins, lags):
    frequency = jnp.arange(bins, dtype=jnp.int32)[None, :]
    lag_offset = jnp.arange(lags, dtype=jnp.int32)[:, None] - lags // 2
    phase_turns = jnp.mod(frequency * lag_offset, 2 * bins).astype(jnp.float32)
    angles = phase_turns * (math.pi / bins)
    return jnp.concatenate([jnp.cos(angles), -jnp.sin(angles)], 1).astype(jnp.bfloat16)


def cos_sin(x):
    square = x * x
    sine, cosine = SINE[-1], COSINE[-1]
    for a, b in zip(SINE[-2::-1], COSINE[-2::-1]):
        sine = sine * square + a
        cosine = cosine * square + b
    sine = sine * x
    return 1.0 - sine * sine, sine * cosine


def flag_column(flags, first):
    lanes = lax.broadcasted_iota(jnp.int32, flags.shape, 1)
    rows = lax.broadcasted_iota(jnp.int32, flags.shape, 0)
    return jnp.sum(jnp.where(lanes == rows + first, flags, 0.0), 1, keepdims=True)


def receivers_kernel(one_ref, two_ref, *out_refs):
    matrix_refs, flag_ref = out_refs[:CHUNKS], out_refs[CHUNKS]
    lanes = lax.broadcasted_iota(jnp.int32, (LANES, LANES), 1)
    for d in range(4):
        block = (one_ref, two_ref)[d // 2]
        marks = jnp.zeros((SRC, LANES), jnp.float32)
        for w in range(WIN_DEV):
            column = flag_column(block[d % 2, w, :, BINS:].astype(jnp.float32), SRC * w)
            marks = marks + jnp.where(lanes[:SRC] == w, column, 0.0)
        flag_ref[SRC * d : SRC * d + SRC, :] = marks.astype(jnp.bfloat16)

    def window(w, carry):
        columns = []
        for d in range(4):
            block = (one_ref, two_ref)[d // 2]
            columns.append(flag_column(block[d % 2, w, :, BINS:].astype(jnp.float32), SRC * w))
        for c in range(CHUNKS):
            real, imag = [], []
            for d in range(4):
                block = (one_ref, two_ref)[d // 2]
                phase = block[d % 2, w, :, LANES * c : LANES * c + LANES].astype(jnp.float32)
                re, im = cos_sin(phase)
                real.append(re * columns[d])
                imag.append(im * columns[d])
            over = jnp.concatenate(real + [-part for part in imag], 0).T
            rows = pl.ds(pl.multiple_of(SRC * w, SRC), SRC)
            for side, values in enumerate((over,)):
                cols = slice(LANES * side, LANES * side + LANES)
                values = values.astype(jnp.bfloat16)
                for k in range(LANES // SRC):
                    matrix_refs[c][k, rows, cols] = values[SRC * k : SRC * k + SRC]
        return carry

    lax.fori_loop(0, WIN_DEV, window, 0)


def receivers(one, two):
    return pl.pallas_call(
        receivers_kernel,
        out_shape=[jax.ShapeDtypeStruct((LANES // SRC, LANES, LANES), jnp.bfloat16)] * CHUNKS
        + [jax.ShapeDtypeStruct((4 * SRC, LANES), jnp.bfloat16)],
        compiler_params=pltpu.CompilerParams(vmem_limit_bytes=12 << 20),
        cost_estimate=pl.CostEstimate(
            flops=25 * 4 * SRC * WIN_DEV * BINS, bytes_accessed=10 << 20, transcendentals=0
        ),
        name="receivers",
    )(one, two)


def correlate_kernel(
    at_ref, src_ref, flag_ref, table_ref, *refs
):
    matrix_refs, (out_ref, by_group, stacked) = refs[:CHUNKS], refs[CHUNKS:]
    lanes = lax.broadcasted_iota(jnp.int32, (SRC, LANES), 1)
    rows = lax.broadcasted_iota(jnp.int32, (SRC, LANES), 0)
    place = at_ref[0]
    every = src_ref[:, BINS:].astype(jnp.float32)
    at = lax.broadcasted_iota(jnp.int32, every.shape, 0) == at_ref[1]
    column = flag_column(
        jnp.broadcast_to(jnp.sum(jnp.where(at, every, 0.0), 0, keepdims=True), every.shape), 0
    )
    marks = jnp.zeros((SRC, LANES), jnp.float32)
    for w in range(WIN_DEV):
        marks = marks + jnp.where(lanes == w, column[SRC * w : SRC * w + SRC], 0.0)
    marks = marks.astype(jnp.bfloat16)

    def prepare(c, carry):
        cols = slice(c * LANES, c * LANES + LANES)
        re, im = cos_sin(src_ref[:, cols].astype(jnp.float32))
        for part, values in enumerate((re * column, im * column)):
            to = slice(2 * SRC * c + SRC * part, 2 * SRC * c + SRC * part + SRC)
            for k in range(LANES // SRC):
                found = None
                for w in range(WIN_DEV):
                    block = values[SRC * w : SRC * w + SRC]
                    shift = SRC * ((w - k) % WIN_DEV)
                    block = pltpu.roll(block, shift, 1) if shift else block
                    found = block if found is None else jnp.where(lanes // SRC == w, block, found)
                by_group[k, to, :] = found
        return carry

    for c in range(CHUNKS):
        prepare(c, 0)
    same_bin = lax.rem(lanes, SRC) == rows
    low = lanes < LANES // 2

    wide = lax.broadcasted_iota(jnp.int32, (LANES, LANES), 1) < LANES // 2
    minus_low = jnp.where(wide, -1.0, 1.0).astype(jnp.bfloat16)
    minus_high = jnp.where(wide, 1.0, -1.0).astype(jnp.bfloat16)
    for chunk in range(CHUNKS):
        for k in range(LANES // SRC):
            group = chunk * (LANES // SRC) + k
            left = []
            for s in range(SRC):
                parts = []
                for part in range(2):
                    row = by_group[k, pl.ds(2 * SRC * chunk + SRC * part + s, 1), :]
                    row = jnp.broadcast_to(row, (SRC, LANES))
                    parts.append(jnp.where(same_bin, row, 0.0).astype(jnp.bfloat16))
                left.append(jnp.concatenate(parts, 1))
            left = jnp.concatenate(left, 0)
            upper = matrix_refs[chunk][k]
            turned = jnp.concatenate([upper[:, LANES // 2 :], upper[:, : LANES // 2]], 1)
            lower = [turned * minus_low, upper * minus_high]
            right = [jnp.concatenate([upper, turned], 1), jnp.concatenate(lower, 1)]
            right = jnp.concatenate(right, 0)
            found = jnp.dot(left, right, preferred_element_type=jnp.float32)
            real = slice(SRC * group, SRC * group + SRC)
            imag = slice(BINS + SRC * group, BINS + SRC * group + SRC)
            for w in range(N_WIN):
                even = found[2 * SRC * w : 2 * SRC * w + SRC]
                odd = found[2 * SRC * w + SRC : 2 * SRC * w + 2 * SRC]
                cols = slice(LANES * w, LANES * w + LANES)
                stacked[real, cols] = jnp.where(low, even[:, :LANES], odd[:, LANES:]).astype(
                    jnp.bfloat16
                )
                stacked[imag, cols] = jnp.where(low, even[:, LANES:], odd[:, :LANES]).astype(
                    jnp.bfloat16
                )
    counts = []
    for d in range(4):
        count = lax.dot_general(
            marks,
            flag_ref[SRC * d : SRC * d + SRC, :],
            (((1,), (1,)), ((), ())),
            preferred_element_type=jnp.float32,
        )
        counts.append(jnp.concatenate([count, jnp.zeros((SRC, LANES - SRC), jnp.float32)], 1))
    for pair in range(0, N_WIN, 2):
        cols = slice(LANES * pair, LANES * pair + 2 * LANES)
        lags = jnp.dot(table_ref[...], stacked[:, cols], preferred_element_type=jnp.float32)
        for w in range(pair, pair + 2):
            first = LANES * (w - pair)
            turned = lags[:, first : first + LANES].T.astype(jnp.bfloat16)
            for d in range(4):
                to = place ^ MASKS[d]
                for s in range(2):
                    part = turned[4 * SRC * s + SRC * d : 4 * SRC * s + SRC * d + SRC]
                    out_ref[w, to, SRC * s : SRC * s + SRC, :] = part[:, :LANES]
                    out_ref[w, to, 2 * SRC + SRC * s : 3 * SRC + SRC * s, :] = part[:, LANES:]
                pair_counts = [counts[d][2 * w : 2 * w + 2], jnp.zeros((6, LANES), jnp.float32)]
                pair_counts = jnp.concatenate(pair_counts, 0).astype(jnp.bfloat16)
                out_ref[w, to, 64:PIECE_ROWS, :] = pair_counts


def correlate(at, source, matrices, rec_flags, table):
    vmem = pl.BlockSpec(memory_space=pltpu.VMEM)
    return pl.pallas_call(
        correlate_kernel,
        out_shape=jax.ShapeDtypeStruct((N_WIN, 4, PIECE_ROWS, LANES), jnp.bfloat16),
        in_specs=[pl.BlockSpec(memory_space=pltpu.SMEM)] + [vmem] * (3 + CHUNKS),
        out_specs=vmem,
        scratch_shapes=[
            pltpu.VMEM((LANES // SRC, 2 * SRC * CHUNKS, LANES), jnp.float32),
            pltpu.VMEM((2 * BINS, SRC * 4 * SRC), jnp.bfloat16),
        ],
        compiler_params=pltpu.CompilerParams(vmem_limit_bytes=20 << 20),
        cost_estimate=pl.CostEstimate(flops=1 << 30, bytes_accessed=12 << 20, transcendentals=0),
        name="correlate",
    )(at, source, rec_flags, table, *matrices)


def on_device(phases, validity, plan):
    me = lax.axis_index("sta")
    place = 2 * (me // 32) + lax.rem(me, 2)
    pieces = lax.all_to_all(
        phases.reshape(N_Z, 8, BINS), "sta", 0, 0, tiled=True, axis_index_groups=ALONG_Z
    )

    flags = validity.astype(jnp.bfloat16).reshape(1, 1, LANES)
    own = jnp.concatenate([phases, jnp.broadcast_to(flags, (WIN_DEV, SRC, LANES))], -1)
    across = lax.ppermute(own, "sta", xor_pairs(32))
    pieces, across = lax.optimization_barrier((pieces, across))
    one = jnp.stack([own, across], 0)
    two = lax.ppermute(one, "sta", xor_pairs(1))
    *matrices, rec_flags = receivers(one, two)

    owner_z = lax.rem(plan // 2, N_Z)
    held = jnp.stack(
        [lax.dynamic_index_in_dim(pieces, owner_z[k], 0, False) for k in range(STEPS)]
    )
    held = jnp.concatenate([held, jnp.broadcast_to(flags, (STEPS, 8, LANES))], -1)
    came = lax.all_to_all(held, "sta", 0, 0, tiled=True, axis_index_groups=QUAD)
    owner = plan[place]
    owner_place = 2 * (owner // 32) + lax.rem(owner, 2)
    sent = lax.dynamic_index_in_dim(came, owner_place, 0, False)
    source = lax.all_to_all(
        jnp.broadcast_to(sent[None], (N_Z, 8, WIDTH)),
        "sta",
        0,
        0,
        tiled=True,
        axis_index_groups=ALONG_Z,
    ).reshape(WIN_DEV * SRC, WIDTH)
    flag_row = 8 * lax.rem(owner // 2, N_Z)

    sent = correlate(
        jnp.stack([place, flag_row]), source, matrices, rec_flags, idft_table(BINS, LAGS)
    )
    back = lax.all_to_all(
        sent.reshape(N_WIN * 4, PIECE_ROWS, LANES),
        ("win", "sta"),
        0,
        0,
        tiled=True,
        axis_index_groups=ALL_QUADS,
    )
    total = jnp.sum(back.reshape(N_WIN, 4, PIECE_ROWS, LANES).astype(jnp.float32), 0)
    lag_sum = total[:, :64].reshape(STEPS, 2, 2, SRC, LANES).transpose(0, 2, 3, 1, 4)
    lag_sum = lag_sum.reshape(STEPS, 2, SRC, LAGS)
    pair_count = total[:, 64:66, :SRC]
    factor = 1.0 / (math.sqrt(BINS) * jnp.sqrt(jnp.maximum(pair_count, 1.0)))
    return (lag_sum * factor[..., None]).astype(jnp.bfloat16)


def solution(mesh):
    return jax.shard_map(
        on_device,
        mesh=mesh,
        in_specs=(P("win", "sta", None), P("win", "sta"), P()),
        out_specs=P(None, "win", "sta", None),
        check_vma=False,
    )
```
